32 devices in a mesh: group: 2 (over x), row: 16 (over z, y, core).
Axes of the slice: x: 2, y: 2, z: 4, core: 2. Of those that a mesh axis runs over, the one named last changes fastest.
Arguments:
- pair_input: bfloat16 [256, 128, 128], P(('group', 'row')), parts along dimension 0, may hold values from -6 to 6
- tri_projection: bfloat16 [128, 512], replicated, may hold values from -0.5 to 0.5
- tri_gate_weight: bfloat16 [128, 128], replicated, may hold values from -0.5 to 0.5
- tri_out_weight: bfloat16 [128, 128], replicated, may hold values from -0.5 to 0.5
- pair_bias_weight: bfloat16 [128, 4], replicated
- atom_input: bfloat16 [2048, 128], P(('group', 'row')), parts along dimension 0, may hold values from -6 to 6
- atom_tokens: int32 [2048], P('group'), parts along dimension 0, may hold values from 0 to 127, as said below
- atom_in_weight: bfloat16 [128, 512], replicated, may hold values from -0.5 to 0.5
- atom_out_weight: bfloat16 [128, 128], replicated, may hold values from -0.5 to 0.5
Outputs:
- pair_output: bfloat16 [256, 128, 128], P(('group', 'row')), parts along dimension 0
- atom_output: bfloat16 [2048, 128], P(('group', 'row')), parts along dimension 0
The draws below stay inside these ranges and needn't reach their ends.
There are 2 independent parts, one for each index of `group`. The reference program is written for one: setup_inputs(seed, part) draws one part's arguments, and reference() takes and returns one part's arrays. A program takes and returns all parts, laid end to end along the dimension named above; an argument that names none is the same for every part. Nothing has to cross between parts.
Inputs may be any that keep to these rules, and one draw needn't show every extreme that they name: `atom_tokens`: never falls along the atoms; atoms 64 q to 64 q + 63 belong to tokens 8 q to 8 q + 7, each of these tokens has 1 to 24 of them.
All inputs are finite; a program needn't handle non-finite values.
Results may differ from the reference program's by a relative error of at most 0.012.
Values may be sent and summed in bfloat16 or wider, within the bound.
A program may use at most 192 MiB of HBM per device.

```python
import jax
import jax.numpy as jnp
from jax import lax

C = 128
CA = 128
H = 4
DH = 32
QB = 32
KB = 128
RIM = 48
MOST = 24
ROWS_DEV = 8
ATOM_DEV = 64
N = 128
NA = 1024


def draw_pair_bias_weight(key, part):
    key = jax.random.fold_in(key, 7)
    values = jax.random.truncated_normal(key, -4.0, 4.0, (C, H), jnp.float32) * (1.5 * C ** (-0.5))
    return values.astype(jnp.bfloat16)


def draw_atom_tokens(key, part):
    key = jax.random.fold_in(key, 11)
    owners = N // ROWS_DEV
    short_len = ATOM_DEV // ROWS_DEV
    long_len = (ATOM_DEV + ROWS_DEV - 1) // ROWS_DEV
    jitter = max(0, min((MOST - long_len) // 2, (short_len - 1) // 2))
    cut_index = jnp.arange(1, ROWS_DEV, dtype=jnp.int32)
    base_cuts = cut_index * ATOM_DEV // ROWS_DEV
    moves = jax.random.randint(key, (owners, ROWS_DEV - 1), -jitter, jitter + 1, jnp.int32)
    cuts = base_cuts[None, :] + moves
    local_atoms = jnp.arange(ATOM_DEV, dtype=jnp.int32)
    within = jnp.sum((local_atoms[None, :, None] >= cuts[:, None, :]).astype(jnp.int32), axis=-1)
    owner_ids = jnp.arange(owners, dtype=jnp.int32)[:, None] * ROWS_DEV
    return (owner_ids + within).reshape(NA).astype(jnp.int32)


def shard_levels(stream_key, shape, split, least, top_value):
    level, own = 1.0, jax.random.fold_in(stream_key, 6)
    for position, shards_of in split:
        steps = jnp.exp(jax.random.uniform(jax.random.fold_in(own, position), (shards_of,), jnp.float32, least / len(split), top_value / len(split)))
        level = level * jnp.repeat(steps, shape[position] // shards_of).reshape([-1 if axis == position else 1 for axis in range(len(shape))])
    return level


def gaussian(rng, shape, deviation, reach, shards=(), kind=jnp.bfloat16):
    level = shard_levels(rng, shape, shards, -0.22, 0.18) if shards else 1.0
    entries = jax.random.normal(rng, shape, jnp.float32) * deviation * level
    return jnp.minimum(jnp.maximum(entries, -reach), reach).astype(kind)


def setup_inputs(seed: int = 0, part: int = 0) -> dict:
    seeds = jax.random.split(jax.random.key(seed), 10)
    own_keys = jax.random.split(jax.random.fold_in(seeds[9], part), 10)
    pair_input = gaussian(own_keys[0], (N, N, C), 1.0, 6.0, ((0, 16),))
    tri_projection = gaussian(seeds[1], (C, 4 * C), C ** -0.5, 0.5)
    tri_gate_weight = gaussian(seeds[2], (C, C), C ** -0.5, 0.5)
    tri_out_weight = gaussian(seeds[3], (C, C), C ** -0.5, 0.5)
    pair_bias_weight = draw_pair_bias_weight(jax.random.fold_in(seeds[9], 71), part)
    atom_input = gaussian(own_keys[5], (NA, CA), 1.0, 6.0, ((0, 16),))
    atom_tokens = draw_atom_tokens(jax.random.fold_in(jax.random.fold_in(seeds[9], part), 71), part)
    atom_in_weight = gaussian(seeds[7], (CA, 4 * CA), CA ** -0.5, 0.5)
    atom_out_weight = gaussian(seeds[8], (CA, CA), CA ** -0.5, 0.5)
    return {"pair_input": pair_input, "tri_projection": tri_projection, "tri_gate_weight": tri_gate_weight, "tri_out_weight": tri_out_weight, "pair_bias_weight": pair_bias_weight, "atom_input": atom_input, "atom_tokens": atom_tokens, "atom_in_weight": atom_in_weight, "atom_out_weight": atom_out_weight}


def layer_norm(values, axis):
    average = lax.optimization_barrier(jnp.mean(values, axis=axis, keepdims=True))
    centred = values - average
    variance = lax.optimization_barrier(jnp.mean(centred * centred, axis=axis, keepdims=True))
    return centred * lax.rsqrt(variance + 1e-05)

def rounded(values):
    return lax.optimization_barrier(values.astype(jnp.bfloat16)).astype(jnp.float32)

def windows(blocked, count):
    return jnp.concatenate([blocked[offset:offset + count] for offset in range(KB // QB)], axis=1)

def reference(pair_input, tri_projection, tri_gate_weight, tri_out_weight, pair_bias_weight, atom_input, atom_tokens, atom_in_weight, atom_out_weight):
    normed = rounded(layer_norm(pair_input.astype(jnp.float32), -1))
    projected = jnp.einsum('kid,de->kie', normed, tri_projection.astype(jnp.float32))
    left_side = rounded(jax.nn.sigmoid(projected[..., C:2 * C]) * projected[..., :C])
    right_side = rounded(jax.nn.sigmoid(projected[..., 3 * C:]) * projected[..., 2 * C:3 * C])
    gate_out = jax.nn.sigmoid(jnp.einsum('kid,de->kie', normed, tri_gate_weight.astype(jnp.float32)))
    triangle = jnp.einsum('kic,kjc->ijc', left_side, right_side)
    tri_normed = rounded(layer_norm(triangle, -1))
    update = jnp.einsum('ijc,cd->ijd', tri_normed, tri_out_weight.astype(jnp.float32))
    pair_output = (pair_input.astype(jnp.float32) + gate_out * update).astype(jnp.bfloat16)
    pair_normed = rounded(layer_norm(pair_output.astype(jnp.float32), -1))
    bias_table = jnp.einsum('ijc,ch->hij', pair_normed, pair_bias_weight.astype(jnp.float32))
    atom_count = atom_input.shape[0]
    block_count = atom_count // QB
    atom_normed = rounded(layer_norm(atom_input.astype(jnp.float32), -1))
    atom_proj = jnp.dot(atom_normed, atom_in_weight.astype(jnp.float32))
    queries = rounded(atom_proj[:, :CA] * DH ** (-0.5)).reshape(block_count, QB, H, DH)
    key_value = rounded(atom_proj[:, CA:3 * CA])
    gating = jax.nn.sigmoid(atom_proj[:, 3 * CA:])
    padded = jnp.pad(key_value, ((RIM, RIM), (0, 0))).reshape(-1, QB, 2 * CA)
    key_windows = windows(padded, block_count)
    keys = key_windows[:, :, :CA].reshape(block_count, KB, H, DH)
    values_win = key_windows[:, :, CA:].reshape(block_count, KB, H, DH)
    positions = jnp.arange(atom_count + 2 * RIM, dtype=jnp.int32) - RIM
    inside = windows(((positions >= 0) & (positions < atom_count)).reshape(-1, QB), block_count)
    clipped = jnp.clip(positions, 0, atom_count - 1).astype(jnp.int32)
    key_tokens = windows(jnp.take(atom_tokens, clipped).reshape(-1, QB), block_count)
    query_tokens = atom_tokens.reshape(block_count, QB)
    bias = bias_table[:, query_tokens[:, :, None], key_tokens[:, None, :]]
    bias = jnp.transpose(bias, (1, 0, 2, 3))
    scores = jnp.einsum('blhd,bmhd->bhlm', queries, keys) + bias
    scores = jnp.where(inside[:, None, None, :], scores, -jnp.inf)
    maxima = lax.optimization_barrier(jnp.max(scores, axis=-1, keepdims=True))
    powers = jnp.exp(scores - maxima)
    weights = rounded(powers / lax.optimization_barrier(jnp.sum(powers, axis=-1, keepdims=True)))
    attended = jnp.einsum('bhlm,bmhd->blhd', weights, values_win).reshape(atom_count, CA)
    gated = rounded(gating * attended)
    atom_output = (jnp.dot(gated, atom_out_weight.astype(jnp.float32)) + atom_input.astype(jnp.float32)).astype(jnp.bfloat16)
    return (pair_output, atom_output)
```

```python
import functools

import jax
import jax.numpy as jnp
from jax import lax
from jax.experimental import pallas as pl
from jax.experimental.pallas import tpu as pltpu
from jax.sharding import PartitionSpec as P

QB = 32
KB = 128
RIM = 48
LANES = 128
NORM_EPSILON = 1e-05
F32 = jnp.float32
BF16 = jnp.bfloat16
NN = (((1,), (0,)), ((), ()))
NT = (((1,), (1,)), ((), ()))


def dot(a, b, dims=NN):
    return lax.dot_general(a, b, dims, preferred_element_type=F32)


def turned(x):
    return jnp.transpose(x.astype(F32)).astype(BF16)


def layer_norm(values, axis):
    average = jnp.mean(values, axis=axis, keepdims=True)
    centred = values - average
    variance = jnp.mean(centred * centred, axis=axis, keepdims=True)
    return centred * lax.rsqrt(variance + NORM_EPSILON)


def kernel(
    count,
    total_atoms,
    pair_ref,
    proj_ref,
    gate_ref,
    out_ref,
    bias_ref,
    atom_ref,
    qtok_ref,
    ktok_ref,
    ain_ref,
    aout_ref,
    pair_out,
    atom_out,
    flat_l,
    flat_r,
    send1,
    recv1,
    send2,
    recv2,
    gates,
    ext,
    ssem1,
    rsem1,
    ssem2,
    rsem2,
    hsem_s,
    hsem_r,
):
    rows, tokens, width = pair_ref.shape
    share = width // count
    part = share * rows
    chunks = tokens // LANES
    atoms = atom_ref.shape[0]
    heads = bias_ref.shape[1]
    head_size = width // heads
    blocks = atoms // QB
    me = lax.axis_index("row")
    right = lax.rem(me + 1, count)
    left = lax.rem(me + count - 1, count)

    barrier = pltpu.get_barrier_semaphore()

    def greet(step, carry):
        pl.semaphore_signal(barrier, inc=1, device_id={"row": lax.rem(me + step, count)})
        return carry

    lax.fori_loop(1, count, greet, 0)

    turned_proj = turned(proj_ref[...])
    for k in range(rows):
        normed = layer_norm(pair_ref[k].astype(F32), -1).astype(BF16)
        projected = dot(turned_proj, normed, NT)
        left_side = jax.nn.sigmoid(projected[width : 2 * width]) * projected[:width]
        right_side = jax.nn.sigmoid(projected[3 * width :]) * projected[2 * width : 3 * width]
        for q in range(chunks):
            cut = slice(q * LANES, (q + 1) * LANES)
            flat_l[q, pl.ds(k, width, stride=rows), :] = left_side[:, cut]
            flat_r[q, pl.ds(k, width, stride=rows), :] = right_side[:, cut]
    for q in range(chunks):
        cut = slice(q * LANES, (q + 1) * LANES)
        send1[:, :part, cut] = flat_l[q].reshape(count, part, LANES).astype(BF16)
        send1[:, part:, cut] = flat_r[q].reshape(count, part, LANES).astype(BF16)

    pl.semaphore_wait(barrier, count - 1)

    def halo(side):
        source = atom_ref.at[pl.ds(atoms - RIM, RIM)] if side == 0 else atom_ref.at[pl.ds(0, RIM)]
        target = ext.at[pl.ds(0, RIM)] if side == 0 else ext.at[pl.ds(RIM + atoms, RIM)]
        return pltpu.make_async_remote_copy(
            src_ref=source,
            dst_ref=target,
            send_sem=hsem_s.at[side],
            recv_sem=hsem_r.at[side],
            device_id={"row": right if side == 0 else left},
        )

    def copy1(peer, slot):
        return pltpu.make_async_remote_copy(
            src_ref=send1.at[peer],
            dst_ref=recv1.at[slot],
            send_sem=ssem1.at[peer],
            recv_sem=rsem1.at[slot],
            device_id={"row": peer},
        )

    def copy2(peer, slot):
        return pltpu.make_async_remote_copy(
            src_ref=send2.at[peer],
            dst_ref=recv2.at[slot],
            send_sem=ssem2.at[peer],
            recv_sem=rsem2.at[slot],
            device_id={"row": peer},
        )

    def start1(step, carry):
        copy1(lax.rem(me + step, count), me).start()
        return carry

    def start2(step, carry):
        copy2(lax.rem(me + step, count), me).start()
        return carry

    def wait1(step, carry):
        peer = lax.rem(me + step, count)
        copy1(peer, peer).wait_recv()
        return carry

    def wait2(step, carry):
        peer = lax.rem(me + step, count)
        copy2(peer, peer).wait_recv()
        return carry

    def drain(step, carry):
        peer = lax.rem(me + step, count)
        copy1(peer, peer).wait_send()
        copy2(peer, peer).wait_send()
        return carry

    halo(0).start()
    halo(1).start()
    lax.fori_loop(1, count, start1, 0)
    recv1[me] = send1[me]
    ext[pl.ds(RIM, atoms), :] = atom_ref[...]

    for k in range(rows):
        normed = layer_norm(pair_ref[k].astype(F32), -1).astype(BF16)
        gates[k] = jax.nn.sigmoid(dot(normed, gate_ref[...]))

    halo(0).wait()
    halo(1).wait()
    reach = atoms + 2 * RIM
    atom_normed = layer_norm(ext[...].astype(F32), -1).astype(BF16)
    atom_proj = dot(atom_normed, ain_ref[...])
    own = atom_proj[RIM : RIM + atoms]
    queries = (own[:, :width] * head_size ** (-0.5)).astype(BF16)
    gating = jax.nn.sigmoid(own[:, 3 * width :])
    keys = atom_proj[:, width : 2 * width].astype(BF16)
    vals = atom_proj[:, 2 * width : 3 * width].astype(BF16)
    channel = lax.broadcasted_iota(jnp.int32, (QB, width), 1) // head_size
    first_atom = me * atoms
    key_tokens = ktok_ref[...]
    query_tokens = qtok_ref[...]
    key_hot = (lax.broadcasted_iota(jnp.int32, (tokens, reach), 0) == key_tokens).astype(BF16)
    base = []
    spread = []
    for b in range(blocks):
        q_b = queries[b * QB : (b + 1) * QB]
        q_all = jnp.concatenate(
            [jnp.where(channel == h, q_b, jnp.zeros_like(q_b)) for h in range(heads)], axis=0
        )
        scores = dot(q_all, keys[b * QB : b * QB + KB], NT)
        position = (
            first_atom
            + (b * QB - RIM)
            + lax.broadcasted_iota(jnp.int32, (heads * QB, KB), 1)
        )
        inside = (position >= 0) & (position < total_atoms)
        base.append(jnp.where(inside, scores, -jnp.inf))
        row = lax.broadcasted_iota(jnp.int32, (2 * heads * rows, heads * QB), 0)
        col = lax.broadcasted_iota(jnp.int32, (2 * heads * rows, heads * QB), 1)
        wanted = (row % rows) == query_tokens[:, b * heads * QB : (b + 1) * heads * QB] - me * rows
        same = ((row // rows) % heads) == col // QB
        spread.append(jnp.transpose((wanted & same).astype(F32)).astype(BF16))

    lax.fori_loop(1, count, wait1, 0)
    step = max(1, 16 // rows)
    for p in range(part // 16):
        at_l = recv1[:, p * 16 : p * 16 + 16, :].astype(F32)
        at_r = recv1[:, part + p * 16 : part + p * 16 + 16, :].astype(F32)
        pieces = []
        for s in range(step):
            cut = slice(s * rows, (s + 1) * rows)
            l_c = at_l[:, cut].reshape(tokens, tokens)
            r_c = at_r[:, cut].reshape(tokens, tokens).astype(BF16)
            tri = dot(jnp.transpose(l_c).astype(BF16), r_c)
            pieces.append(tri.reshape(count, rows, tokens))
        send2[:, p * 16 : p * 16 + 16, :] = jnp.concatenate(pieces, axis=1).astype(BF16)
    lax.fori_loop(1, count, start2, 0)
    recv2[me] = send2[me]
    lax.fori_loop(1, count, wait2, 0)

    for q in range(chunks):
        cut = slice(q * LANES, (q + 1) * LANES)
        triangle = recv2[:, :, cut].astype(F32).reshape(width, rows, LANES)
        flat_l[q] = layer_norm(triangle, 0).reshape(width * rows, LANES)
    turned_bias = turned(bias_ref[...])
    bias_rows = []
    for k in range(rows):
        for q in range(chunks):
            cut = slice(q * LANES, (q + 1) * LANES)
            tri_normed = flat_l[q, pl.ds(k, width, stride=rows), :]
            update = dot(jnp.transpose(tri_normed).astype(BF16), out_ref[...])
            result = (pair_ref[k, cut].astype(F32) + gates[k, cut] * update).astype(BF16)
            pair_out[k, cut] = result
            pair_normed = layer_norm(result.astype(F32), -1).astype(BF16)
            bias_rows.append(dot(turned_bias, pair_normed, NT))
    table = jnp.stack(
        [
            jnp.concatenate(bias_rows[k * chunks : (k + 1) * chunks], axis=1)
            for k in range(rows)
        ],
        axis=1,
    ).reshape(heads * rows, tokens)
    high = table.astype(BF16)
    low = (table - high.astype(F32)).astype(BF16)
    both = dot(jnp.concatenate([high, low], axis=0), key_hot).astype(BF16)
    parts = []
    for b in range(blocks):
        scores = base[b] + dot(spread[b], both[:, b * QB : b * QB + KB])
        powers = jnp.exp(scores - jnp.max(scores, axis=-1, keepdims=True))
        weights = (powers / jnp.sum(powers, axis=-1, keepdims=True)).astype(BF16)
        every = dot(weights, vals[b * QB : b * QB + KB])
        attended = jnp.zeros((QB, width), F32)
        for h in range(heads):
            attended = jnp.where(channel == h, every[h * QB : (h + 1) * QB], attended)
        parts.append(attended)
    gated = (gating * jnp.concatenate(parts, axis=0)).astype(BF16)
    atom_out[...] = (dot(gated, aout_ref[...]) + atom_ref[...].astype(F32)).astype(BF16)
    lax.fori_loop(1, count, drain, 0)


def per_device(
    count,
    pair_input,
    tri_projection,
    tri_gate_weight,
    tri_out_weight,
    pair_bias_weight,
    atom_input,
    atom_tokens,
    atom_in_weight,
    atom_out_weight,
):
    rows, tokens, width = pair_input.shape
    atoms = atom_input.shape[0]
    heads = pair_bias_weight.shape[1]
    share = width // count
    part = share * rows
    chunks = tokens // LANES
    total_atoms = atom_tokens.shape[0]
    first_atom = lax.axis_index("row") * atoms
    padded_tokens = jnp.pad(atom_tokens, RIM)
    key_tokens = lax.dynamic_slice_in_dim(padded_tokens, first_atom, atoms + 2 * RIM)[None]
    query_tokens = lax.dynamic_slice_in_dim(atom_tokens, first_atom, atoms)
    query_tokens = jnp.tile(query_tokens.reshape(-1, 1, QB), (1, heads, 1)).reshape(1, -1)
    vmem = pl.BlockSpec(memory_space=pltpu.VMEM)
    return pl.pallas_call(
        functools.partial(kernel, count, total_atoms),
        out_shape=(
            jax.ShapeDtypeStruct(pair_input.shape, BF16),
            jax.ShapeDtypeStruct(atom_input.shape, BF16),
        ),
        in_specs=[vmem] * 10,
        out_specs=(vmem, vmem),
        scratch_shapes=[
            pltpu.VMEM((chunks, width * rows, LANES), F32),
            pltpu.VMEM((chunks, width * rows, LANES), F32),
            pltpu.VMEM((count, 2 * part, tokens), BF16),
            pltpu.VMEM((count, 2 * part, tokens), BF16),
            pltpu.VMEM((count, part, tokens), BF16),
            pltpu.VMEM((count, part, tokens), BF16),
            pltpu.VMEM((rows, tokens, width), F32),
            pltpu.VMEM((atoms + 2 * RIM, width), BF16),
            pltpu.SemaphoreType.DMA((count,)),
            pltpu.SemaphoreType.DMA((count,)),
            pltpu.SemaphoreType.DMA((count,)),
            pltpu.SemaphoreType.DMA((count,)),
            pltpu.SemaphoreType.DMA((2,)),
            pltpu.SemaphoreType.DMA((2,)),
        ],
        compiler_params=pltpu.CompilerParams(
            collective_id=0, has_side_effects=True, vmem_limit_bytes=40 * 1024 * 1024
        ),
    )(
        pair_input,
        tri_projection,
        tri_gate_weight,
        tri_out_weight,
        pair_bias_weight,
        atom_input,
        query_tokens,
        key_tokens,
        atom_in_weight,
        atom_out_weight,
    )


def solution(mesh):
    placed = (
        P(("group", "row"), None, None),
        P(),
        P(),
        P(),
        P(),
        P(("group", "row"), None),
        P("group"),
        P(),
        P(),
    )
    return jax.shard_map(
        functools.partial(per_device, mesh.shape["row"]),
        mesh=mesh,
        in_specs=placed,
        out_specs=(P(("group", "row"), None, None), P(("group", "row"), None)),
        check_vma=False,
    )
```

```python
import functools

import jax
import jax.numpy as jnp
from jax import lax
from jax.experimental import pallas as pl
from jax.experimental.pallas import tpu as pltpu
from jax.sharding import PartitionSpec as P

QB = 32
KB = 128
RIM = 48
LANES = 128
NORM_EPSILON = 1e-05
F32 = jnp.float32
BF16 = jnp.bfloat16
NN = (((1,), (0,)), ((), ()))
NT = (((1,), (1,)), ((), ()))


def dot(a, b, dims=NN):
    return lax.dot_general(a, b, dims, preferred_element_type=F32)


def turned(x):
    return jnp.transpose(x.astype(F32)).astype(BF16)


def layer_norm(values, axis):
    average = jnp.mean(values, axis=axis, keepdims=True)
    centred = values - average
    variance = jnp.mean(centred * centred, axis=axis, keepdims=True)
    return centred * lax.rsqrt(variance + NORM_EPSILON)


def kernel(
    count,
    groups,
    total_atoms,
    pair_hbm,
    proj_hbm,
    gate_hbm,
    out_hbm,
    bias_ref,
    atom_hbm,
    tok_hbm,
    ain_hbm,
    aout_hbm,
    pair_out,
    atom_out,
    pair_ref,
    proj_ref,
    gate_ref,
    out_ref,
    tok_ref,
    ain_ref,
    aout_ref,
    normed_ref,
    flat_l,
    flat_r,
    send1,
    recv1,
    send2,
    recv2,
    gates,
    ext,
    ssem1,
    rsem1,
    ssem2,
    rsem2,
    hsem_s,
    hsem_r,
    isem,
):
    rows, tokens, width = pair_ref.shape
    share = width // count
    part = share * rows // groups
    held = width // groups
    chunks = tokens // LANES
    atoms = ext.shape[0] - 2 * RIM
    reach = atoms + 2 * RIM
    heads = bias_ref.shape[0]
    head_size = width // heads
    blocks = atoms // QB
    token_rows = total_atoms // LANES
    me = lax.axis_index("row")
    right = lax.rem(me + 1, count)
    left = lax.rem(me + count - 1, count)
    cuts = [slice(q * LANES, (q + 1) * LANES) for q in range(chunks)]

    barrier = pltpu.get_barrier_semaphore()

    def greet(step, carry):
        pl.semaphore_signal(barrier, inc=1, device_id={"row": lax.rem(me + step, count)})
        return carry

    lax.fori_loop(1, count, greet, 0)

    fetches = [
        pltpu.make_async_copy(source, target, isem.at[i])
        for i, (source, target) in enumerate(
            [
                (pair_hbm, pair_ref),
                (proj_hbm, proj_ref),
                (gate_hbm, gate_ref),
                (out_hbm, out_ref),
                (atom_hbm, ext.at[pl.ds(RIM, atoms)]),
                (tok_hbm, tok_ref.at[pl.ds(8, token_rows)]),
                (ain_hbm, ain_ref),
                (aout_hbm, aout_ref),
            ]
        )
    ]
    for fetch in fetches:
        fetch.start()
    tok_ref[pl.ds(0, 8), :] = jnp.zeros((8, LANES), jnp.int32)
    tok_ref[pl.ds(8 + token_rows, 8), :] = jnp.zeros((8, LANES), jnp.int32)

    def peer_of(step):
        return lax.rem(me + lax.rem(step + count // 2 - 2, count - 1) + 1, count)

    def halo(side):
        source = atom_hbm.at[pl.ds(atoms - RIM, RIM)] if side == 0 else atom_hbm.at[pl.ds(0, RIM)]
        target = ext.at[pl.ds(0, RIM)] if side == 0 else ext.at[pl.ds(RIM + atoms, RIM)]
        return pltpu.make_async_remote_copy(
            src_ref=source,
            dst_ref=target,
            send_sem=hsem_s.at[side],
            recv_sem=hsem_r.at[side],
            device_id={"row": right if side == 0 else left},
        )

    def copy1(g, peer, slot):
        return pltpu.make_async_remote_copy(
            src_ref=send1.at[g, peer],
            dst_ref=recv1.at[g, slot],
            send_sem=ssem1.at[g, peer],
            recv_sem=rsem1.at[g, slot],
            device_id={"row": peer},
        )

    def copy2(g, peer, slot):
        return pltpu.make_async_remote_copy(
            src_ref=send2.at[g, peer],
            dst_ref=recv2.at[g, slot],
            send_sem=ssem2.at[g, peer],
            recv_sem=rsem2.at[g, slot],
            device_id={"row": peer},
        )

    def start(copy, g):
        def body(step, carry):
            copy(g, peer_of(step), me).start()
            return carry

        lax.fori_loop(1, count, body, 0)

    def arrive(copy, g):
        def body(step, carry):
            peer = peer_of(step)
            copy(g, peer, peer).wait_recv()
            return carry

        lax.fori_loop(1, count, body, 0)

    def leave(copy, g):
        def body(step, carry):
            peer = peer_of(step)
            copy(g, peer, peer).wait_send()
            return carry

        lax.fori_loop(1, count, body, 0)

    fetches[1].wait()
    turned_proj = turned(proj_ref[...])
    fetches[0].wait()
    for g in range(groups):
        sides = [
            turned_proj[t * width + g * held : t * width + (g + 1) * held] for t in range(4)
        ]
        sides = jnp.concatenate(sides, axis=0)
        for k in range(rows):
            if g == 0:
                normed = layer_norm(pair_ref[k].astype(F32), -1).astype(BF16)
                normed_ref[k] = normed
            else:
                normed = normed_ref[k]
            projected = dot(sides, normed, NT)
            left_side = jax.nn.sigmoid(projected[held : 2 * held]) * projected[:held]
            right_side = jax.nn.sigmoid(projected[3 * held :]) * projected[2 * held : 3 * held]
            for q in range(chunks):
                flat_l[q, pl.ds(g * held * rows + k, held, stride=rows), :] = left_side[:, cuts[q]]
                flat_r[q, pl.ds(g * held * rows + k, held, stride=rows), :] = right_side[:, cuts[q]]
        span = pl.ds(g * held * rows, held * rows)
        for q in range(chunks):
            send1[g, :, :part, cuts[q]] = (
                flat_l[q, span, :].reshape(count, part, LANES).astype(BF16)
            )
            send1[g, :, part:, cuts[q]] = (
                flat_r[q, span, :].reshape(count, part, LANES).astype(BF16)
            )
        if g == 0:
            pl.semaphore_wait(barrier, count - 1)
            halo(0).start()
            halo(1).start()
        start(copy1, g)
        recv1[g, me] = send1[g, me]

    fetches[2].wait()
    for k in range(rows):
        gates[k] = jax.nn.sigmoid(dot(normed_ref[k], gate_ref[...]))

    for i in (3, 4, 5, 6, 7):
        fetches[i].wait()
    halo(0).wait()
    halo(1).wait()
    atom_normed = layer_norm(ext[...].astype(F32), -1).astype(BF16)
    atom_proj = dot(atom_normed, ain_ref[...])
    own = atom_proj[RIM : RIM + atoms]
    queries = (own[:, :width] * head_size ** (-0.5)).astype(BF16)
    gating = jax.nn.sigmoid(own[:, 3 * width :])
    keys = atom_proj[:, width : 2 * width].astype(BF16)
    vals = atom_proj[:, 2 * width : 3 * width].astype(BF16)
    channel = lax.broadcasted_iota(jnp.int32, (QB, width), 1) // head_size
    first_atom = me * atoms
    token_row = first_atom // LANES
    around = jnp.concatenate(
        [tok_ref[pl.ds(7 + token_row + t, 1), :] for t in range(3)], axis=1
    )
    key_tokens = around[:, LANES - RIM : LANES - RIM + reach]
    for t in range(1, LANES // atoms):
        begin = LANES - RIM + t * atoms
        key_tokens = jnp.where(
            first_atom % LANES == t * atoms, around[:, begin : begin + reach], key_tokens
        )
    key_hot = (lax.broadcasted_iota(jnp.int32, (tokens, reach), 0) == key_tokens).astype(BF16)
    base = []
    spread = []
    for b in range(blocks):
        q_b = queries[b * QB : (b + 1) * QB]
        q_all = jnp.concatenate(
            [jnp.where(channel == h, q_b, jnp.zeros_like(q_b)) for h in range(heads)], axis=0
        )
        scores = dot(q_all, keys[b * QB : b * QB + KB], NT)
        position = (
            first_atom
            + (b * QB - RIM)
            + lax.broadcasted_iota(jnp.int32, (heads * QB, KB), 1)
        )
        inside = (position >= 0) & (position < total_atoms)
        base.append(jnp.where(inside, scores, -jnp.inf))
        row = lax.broadcasted_iota(jnp.int32, (2 * heads * rows, heads * QB), 0)
        col = lax.broadcasted_iota(jnp.int32, (2 * heads * rows, heads * QB), 1)
        begin = RIM + b * QB
        own_tokens = jnp.concatenate([key_tokens[:, begin : begin + QB]] * heads, axis=1)
        wanted = (row % rows) == own_tokens - me * rows
        same = ((row // rows) % heads) == col // QB
        spread.append(jnp.transpose((wanted & same).astype(F32)).astype(BF16))

    step = 16 // rows
    for g in range(groups):
        arrive(copy1, g)
        for p in range(part // 16):
            at_l = recv1[g, :, p * 16 : p * 16 + 16, :].astype(F32)
            at_r = recv1[g, :, part + p * 16 : part + p * 16 + 16, :].astype(F32)
            pieces = []
            for s in range(step):
                cut = slice(s * rows, (s + 1) * rows)
                l_c = at_l[:, cut].reshape(tokens, tokens)
                r_c = at_r[:, cut].reshape(tokens, tokens).astype(BF16)
                tri = dot(jnp.transpose(l_c).astype(BF16), r_c)
                pieces.append(tri.reshape(count, rows, tokens))
            send2[g, :, p * 16 : p * 16 + 16, :] = jnp.concatenate(pieces, axis=1).astype(BF16)
        start(copy2, g)
        recv2[g, me] = send2[g, me]
    for g in range(groups):
        arrive(copy2, g)

    for q in range(chunks):
        triangle = recv2[:, :, :, cuts[q]].astype(F32).reshape(width, rows, LANES)
        flat_l[q] = layer_norm(triangle, 0).reshape(width * rows, LANES)
    turned_bias = bias_ref[...].astype(BF16)
    bias_rows = []
    for k in range(rows):
        for cut_q in range(chunks):
            cut = cuts[cut_q]
            tri_normed = flat_l[cut_q, pl.ds(k, width, stride=rows), :]
            update = dot(jnp.transpose(tri_normed).astype(BF16), out_ref[...])
            result = (pair_ref[k, cut].astype(F32) + gates[k, cut] * update).astype(BF16)
            pair_out[k, cut] = result
            pair_normed = layer_norm(result.astype(F32), -1).astype(BF16)
            bias_rows.append(dot(turned_bias, pair_normed, NT))
    table = jnp.stack(
        [
            jnp.concatenate(bias_rows[k * chunks : (k + 1) * chunks], axis=1)
            for k in range(rows)
        ],
        axis=1,
    ).reshape(heads * rows, tokens)
    high = table.astype(BF16)
    low = (table - high.astype(F32)).astype(BF16)
    both = dot(jnp.concatenate([high, low], axis=0), key_hot).astype(BF16)
    parts = []
    for b in range(blocks):
        scores = base[b] + dot(spread[b], both[:, b * QB : b * QB + KB])
        powers = jnp.exp(scores - jnp.max(scores, axis=-1, keepdims=True))
        weights = (powers / jnp.sum(powers, axis=-1, keepdims=True)).astype(BF16)
        every = dot(weights, vals[b * QB : b * QB + KB])
        attended = jnp.zeros((QB, width), F32)
        for h in range(heads):
            attended = jnp.where(channel == h, every[h * QB : (h + 1) * QB], attended)
        parts.append(attended)
    gated = (gating * jnp.concatenate(parts, axis=0)).astype(BF16)
    atom_out[...] = (
        dot(gated, aout_ref[...]) + ext[pl.ds(RIM, atoms), :].astype(F32)
    ).astype(BF16)
    for g in range(groups):
        leave(copy1, g)
        leave(copy2, g)


def per_device(
    count,
    pair_input,
    tri_projection,
    tri_gate_weight,
    tri_out_weight,
    pair_bias_weight,
    atom_input,
    atom_tokens,
    atom_in_weight,
    atom_out_weight,
):
    rows, tokens, width = pair_input.shape
    atoms = atom_input.shape[0]
    groups = max(1, width // count * rows // 32)
    part = width // count * rows // groups
    chunks = tokens // LANES
    total_atoms = atom_tokens.shape[0]
    vmem = pl.BlockSpec(memory_space=pltpu.VMEM)
    anywhere = pl.BlockSpec(memory_space=pl.ANY)
    return pl.pallas_call(
        functools.partial(kernel, count, groups, total_atoms),
        out_shape=(
            jax.ShapeDtypeStruct(pair_input.shape, BF16),
            jax.ShapeDtypeStruct(atom_input.shape, BF16),
        ),
        in_specs=[anywhere] * 4 + [vmem] + [anywhere] * 4,
        out_specs=(vmem, vmem),
        scratch_shapes=[
            pltpu.VMEM(pair_input.shape, BF16),
            pltpu.VMEM(tri_projection.shape, BF16),
            pltpu.VMEM(tri_gate_weight.shape, BF16),
            pltpu.VMEM(tri_out_weight.shape, BF16),
            pltpu.VMEM((total_atoms // LANES + 16, LANES), jnp.int32),
            pltpu.VMEM(atom_in_weight.shape, BF16),
            pltpu.VMEM(atom_out_weight.shape, BF16),
            pltpu.VMEM(pair_input.shape, BF16),
            pltpu.VMEM((chunks, width * rows, LANES), F32),
            pltpu.VMEM((chunks, width * rows, LANES), F32),
            pltpu.VMEM((groups, count, 2 * part, tokens), BF16),
            pltpu.VMEM((groups, count, 2 * part, tokens), BF16),
            pltpu.VMEM((groups, count, part, tokens), BF16),
            pltpu.VMEM((groups, count, part, tokens), BF16),
            pltpu.VMEM((rows, tokens, width), F32),
            pltpu.VMEM((atoms + 2 * RIM, width), BF16),
            pltpu.SemaphoreType.DMA((groups, count)),
            pltpu.SemaphoreType.DMA((groups, count)),
            pltpu.SemaphoreType.DMA((groups, count)),
            pltpu.SemaphoreType.DMA((groups, count)),
            pltpu.SemaphoreType.DMA((2,)),
            pltpu.SemaphoreType.DMA((2,)),
            pltpu.SemaphoreType.DMA((8,)),
        ],
        compiler_params=pltpu.CompilerParams(
            collective_id=0, has_side_effects=True, vmem_limit_bytes=60 * 1024 * 1024
        ),
    )(
        pair_input,
        tri_projection,
        tri_gate_weight,
        tri_out_weight,
        pair_bias_weight.T.astype(F32),
        atom_input,
        atom_tokens.reshape(-1, LANES),
        atom_in_weight,
        atom_out_weight,
    )


def solution(mesh):
    placed = (
        P(("group", "row"), None, None),
        P(),
        P(),
        P(),
        P(),
        P(("group", "row"), None),
        P("group"),
        P(),
        P(),
    )
    return jax.shard_map(
        functools.partial(per_device, mesh.shape["row"]),
        mesh=mesh,
        in_specs=placed,
        out_specs=(P(("group", "row"), None, None), P(("group", "row"), None)),
        check_vma=False,
    )
```

```python
import functools

import jax
import jax.numpy as jnp
from jax import lax
from jax.experimental import pallas as pl
from jax.experimental.pallas import tpu as pltpu
from jax.sharding import PartitionSpec as P

QB = 32
KB = 128
RIM = 48
LANES = 128
NORM_EPSILON = 1e-05
F32 = jnp.float32
BF16 = jnp.bfloat16
NN = (((1,), (0,)), ((), ()))
NT = (((1,), (1,)), ((), ()))


def dot(a, b, dims=NN):
    return lax.dot_general(a, b, dims, preferred_element_type=F32)


def turned(x):
    return jnp.transpose(x.astype(F32)).astype(BF16)


def layer_norm(values, axis):
    average = jnp.mean(values, axis=axis, keepdims=True)
    centred = values - average
    variance = jnp.mean(centred * centred, axis=axis, keepdims=True)
    return centred * lax.rsqrt(variance + NORM_EPSILON)


def kernel(
    count,
    groups,
    total_atoms,
    pair_hbm,
    proj_hbm,
    gate_hbm,
    out_hbm,
    bias_hbm,
    atom_hbm,
    tok_hbm,
    ain_hbm,
    aout_hbm,
    pair_to,
    atom_to,
    pair_out,
    atom_out,
    pair_ref,
    proj_ref,
    gate_ref,
    out_ref,
    bias_ref,
    tok_ref,
    ain_ref,
    aout_ref,
    normed_ref,
    flat_l,
    flat_r,
    send1,
    recv1,
    send2,
    recv2,
    gates,
    ext,
    ssem1,
    rsem1,
    ssem2,
    rsem2,
    hsem_s,
    hsem_r,
    isem,
    osem,
):
    rows, tokens, width = pair_ref.shape
    share = width // count
    part = share * rows // groups
    held = width // groups
    chunks = tokens // LANES
    atoms = ext.shape[0] - 2 * RIM
    reach = atoms + 2 * RIM
    heads = bias_ref.shape[0]
    head_size = width // heads
    blocks = atoms // QB
    token_rows = total_atoms // LANES
    me = lax.axis_index("row")
    right = lax.rem(me + 1, count)
    left = lax.rem(me + count - 1, count)
    cuts = [slice(q * LANES, (q + 1) * LANES) for q in range(chunks)]

    barrier = pltpu.get_barrier_semaphore()

    def greet(step, carry):
        pl.semaphore_signal(barrier, inc=1, device_id={"row": lax.rem(me + step, count)})
        return carry

    lax.fori_loop(1, count, greet, 0, unroll=True)

    fetches = [
        pltpu.make_async_copy(source, target, isem.at[i])
        for i, (source, target) in enumerate(
            [
                (pair_hbm, pair_ref),
                (proj_hbm, proj_ref),
                (gate_hbm, gate_ref),
                (out_hbm, out_ref),
                (atom_hbm, ext.at[pl.ds(RIM, atoms)]),
                (tok_hbm, tok_ref.at[pl.ds(8, token_rows)]),
                (ain_hbm, ain_ref),
                (aout_hbm, aout_ref),
                (bias_hbm, bias_ref),
            ]
        )
    ]
    for fetch in fetches:
        fetch.start()
    tok_ref[pl.ds(0, 8), :] = jnp.zeros((8, LANES), jnp.int32)
    tok_ref[pl.ds(8 + token_rows, 8), :] = jnp.zeros((8, LANES), jnp.int32)

    def peer_of(step):
        return lax.rem(me + step, count)

    def halo(side):
        source = atom_hbm.at[pl.ds(atoms - RIM, RIM)] if side == 0 else atom_hbm.at[pl.ds(0, RIM)]
        target = ext.at[pl.ds(0, RIM)] if side == 0 else ext.at[pl.ds(RIM + atoms, RIM)]
        return pltpu.make_async_remote_copy(
            src_ref=source,
            dst_ref=target,
            send_sem=hsem_s.at[side],
            recv_sem=hsem_r.at[side],
            device_id={"row": right if side == 0 else left},
        )

    def copy1(g, peer, slot):
        return pltpu.make_async_remote_copy(
            src_ref=send1.at[g, peer],
            dst_ref=recv1.at[g, slot],
            send_sem=ssem1.at[g],
            recv_sem=rsem1.at[g],
            device_id={"row": peer},
        )

    def copy2(g, peer, slot):
        return pltpu.make_async_remote_copy(
            src_ref=send2.at[g, peer],
            dst_ref=recv2.at[g, slot],
            send_sem=ssem2.at[g],
            recv_sem=rsem2.at[g],
            device_id={"row": peer},
        )

    def start(copy, g):
        def body(step, carry):
            copy(g, peer_of(step), me).start()
            return carry

        lax.fori_loop(1, count, body, 0, unroll=True)

    def all1(g):
        return pltpu.make_async_remote_copy(
            src_ref=send1.at[g, pl.ds(0, count - 1)],
            dst_ref=recv1.at[g, pl.ds(0, count - 1)],
            send_sem=ssem1.at[g],
            recv_sem=rsem1.at[g],
            device_id={"row": right},
        )

    def all2(g):
        return pltpu.make_async_remote_copy(
            src_ref=send2.at[g, pl.ds(0, count - 1)],
            dst_ref=recv2.at[g, pl.ds(0, count - 1)],
            send_sem=ssem2.at[g],
            recv_sem=rsem2.at[g],
            device_id={"row": right},
        )

    fetches[1].wait()
    turned_proj = turned(proj_ref[...])
    fetches[0].wait()
    for g in range(groups):
        sides = [
            turned_proj[t * width + g * held : t * width + (g + 1) * held] for t in range(4)
        ]
        sides = jnp.concatenate(sides, axis=0)
        for k in range(rows):
            if g == 0:
                normed = layer_norm(pair_ref[k].astype(F32), -1).astype(BF16)
                normed_ref[k] = normed
            else:
                normed = normed_ref[k]
            projected = dot(sides, normed, NT)
            left_side = jax.nn.sigmoid(projected[held : 2 * held]) * projected[:held]
            right_side = jax.nn.sigmoid(projected[3 * held :]) * projected[2 * held : 3 * held]
            for q in range(chunks):
                flat_l[q, pl.ds(g * held * rows + k, held, stride=rows), :] = left_side[:, cuts[q]]
                flat_r[q, pl.ds(g * held * rows + k, held, stride=rows), :] = right_side[:, cuts[q]]
        span = pl.ds(g * held * rows, held * rows)
        for q in range(chunks):
            send1[g, :, :part, cuts[q]] = (
                flat_l[q, span, :].reshape(count, part, LANES).astype(BF16)
            )
            send1[g, :, part:, cuts[q]] = (
                flat_r[q, span, :].reshape(count, part, LANES).astype(BF16)
            )
        if g == 0:
            pl.semaphore_wait(barrier, count - 1)
            halo(0).start()
            halo(1).start()
        start(copy1, g)
        recv1[g, me] = send1[g, me]

    fetches[2].wait()
    for k in range(rows):
        gates[k] = jax.nn.sigmoid(dot(normed_ref[k], gate_ref[...]))

    for i in (3, 4, 5, 6, 7, 8):
        fetches[i].wait()
    halo(0).wait()
    halo(1).wait()
    atom_normed = layer_norm(ext[...].astype(F32), -1).astype(BF16)
    atom_proj = dot(atom_normed, ain_ref[...])
    own = atom_proj[RIM : RIM + atoms]
    queries = (own[:, :width] * head_size ** (-0.5)).astype(BF16)
    gating = jax.nn.sigmoid(own[:, 3 * width :])
    keys = atom_proj[:, width : 2 * width].astype(BF16)
    vals = atom_proj[:, 2 * width : 3 * width].astype(BF16)
    channel = lax.broadcasted_iota(jnp.int32, (QB, width), 1) // head_size
    first_atom = me * atoms
    token_row = first_atom // LANES
    around = jnp.concatenate(
        [tok_ref[pl.ds(7 + token_row + t, 1), :] for t in range(3)], axis=1
    )
    key_tokens = around[:, LANES - RIM : LANES - RIM + reach]
    for t in range(1, LANES // atoms):
        begin = LANES - RIM + t * atoms
        key_tokens = jnp.where(
            first_atom % LANES == t * atoms, around[:, begin : begin + reach], key_tokens
        )
    key_hot = (lax.broadcasted_iota(jnp.int32, (tokens, reach), 0) == key_tokens).astype(BF16)
    base = []
    spread = []
    for b in range(blocks):
        q_b = queries[b * QB : (b + 1) * QB]
        q_all = jnp.concatenate(
            [jnp.where(channel == h, q_b, jnp.zeros_like(q_b)) for h in range(heads)], axis=0
        )
        scores = dot(q_all, keys[b * QB : b * QB + KB], NT)
        position = (
            first_atom
            + (b * QB - RIM)
            + lax.broadcasted_iota(jnp.int32, (heads * QB, KB), 1)
        )
        inside = (position >= 0) & (position < total_atoms)
        base.append(jnp.where(inside, scores, -jnp.inf))
        row = lax.broadcasted_iota(jnp.int32, (2 * heads * rows, heads * QB), 0)
        col = lax.broadcasted_iota(jnp.int32, (2 * heads * rows, heads * QB), 1)
        begin = RIM + b * QB
        own_tokens = jnp.concatenate([key_tokens[:, begin : begin + QB]] * heads, axis=1)
        wanted = (row % rows) == own_tokens - me * rows
        same = ((row // rows) % heads) == col // QB
        spread.append(jnp.transpose((wanted & same).astype(F32)).astype(BF16))

    step = 16 // rows
    for g in range(groups):
        all1(g).wait_recv()
        for p in range(part // 16):
            at_l = recv1[g, :, p * 16 : p * 16 + 16, :].astype(F32)
            at_r = recv1[g, :, part + p * 16 : part + p * 16 + 16, :].astype(F32)
            pieces = []
            for s in range(step):
                cut = slice(s * rows, (s + 1) * rows)
                l_c = at_l[:, cut].reshape(tokens, tokens)
                r_c = at_r[:, cut].reshape(tokens, tokens).astype(BF16)
                tri = dot(jnp.transpose(l_c).astype(BF16), r_c)
                pieces.append(tri.reshape(count, rows, tokens))
            send2[g, :, p * 16 : p * 16 + 16, :] = jnp.concatenate(pieces, axis=1).astype(BF16)
        start(copy2, g)
        recv2[g, me] = send2[g, me]
    for g in range(groups):
        all2(g).wait_recv()

    for q in range(chunks):
        triangle = recv2[:, :, :, cuts[q]].astype(F32).reshape(width, rows, LANES)
        flat_l[q] = layer_norm(triangle, 0).reshape(width * rows, LANES)
    turned_bias = bias_ref[...]
    bias_rows = []
    stores = []
    for k in range(rows):
        for cut_q in range(chunks):
            cut = cuts[cut_q]
            tri_normed = flat_l[cut_q, pl.ds(k, width, stride=rows), :]
            update = dot(jnp.transpose(tri_normed).astype(BF16), out_ref[...])
            result = (pair_ref[k, cut].astype(F32) + gates[k, cut] * update).astype(BF16)
            pair_out[k, cut] = result
            pair_normed = layer_norm(result.astype(F32), -1).astype(BF16)
            bias_rows.append(dot(turned_bias, pair_normed, NT))
        stores.append(pltpu.make_async_copy(pair_out.at[k], pair_to.at[k], osem.at[k]))
        stores[-1].start()
    table = jnp.stack(
        [
            jnp.concatenate(bias_rows[k * chunks : (k + 1) * chunks], axis=1)
            for k in range(rows)
        ],
        axis=1,
    ).reshape(heads * rows, tokens)
    high = table.astype(BF16)
    low = (table - high.astype(F32)).astype(BF16)
    both = dot(jnp.concatenate([high, low], axis=0), key_hot).astype(BF16)
    parts = []
    for b in range(blocks):
        scores = base[b] + dot(spread[b], both[:, b * QB : b * QB + KB])
        powers = jnp.exp(scores - jnp.max(scores, axis=-1, keepdims=True))
        weights = (powers / jnp.sum(powers, axis=-1, keepdims=True)).astype(BF16)
        every = dot(weights, vals[b * QB : b * QB + KB])
        attended = jnp.zeros((QB, width), F32)
        for h in range(heads):
            attended = jnp.where(channel == h, every[h * QB : (h + 1) * QB], attended)
        parts.append(attended)
    gated = (gating * jnp.concatenate(parts, axis=0)).astype(BF16)
    atom_out[...] = (
        dot(gated, aout_ref[...]) + ext[pl.ds(RIM, atoms), :].astype(F32)
    ).astype(BF16)
    stores.append(pltpu.make_async_copy(atom_out, atom_to, osem.at[rows]))
    stores[-1].start()
    for g in range(groups):
        all1(g).wait_send()
        all2(g).wait_send()
    for store in stores:
        store.wait()


def per_device(
    count,
    pair_input,
    tri_projection,
    tri_gate_weight,
    tri_out_weight,
    pair_bias_weight,
    atom_input,
    atom_tokens,
    atom_in_weight,
    atom_out_weight,
):
    rows, tokens, width = pair_input.shape
    atoms = atom_input.shape[0]
    groups = 1
    part = width // count * rows // groups
    chunks = tokens // LANES
    total_atoms = atom_tokens.shape[0]
    anywhere = pl.BlockSpec(memory_space=pl.ANY)
    return pl.pallas_call(
        functools.partial(kernel, count, groups, total_atoms),
        out_shape=(
            jax.ShapeDtypeStruct(pair_input.shape, BF16),
            jax.ShapeDtypeStruct(atom_input.shape, BF16),
        ),
        in_specs=[anywhere] * 9,
        out_specs=(anywhere, anywhere),
        scratch_shapes=[
            pltpu.VMEM(pair_input.shape, BF16),
            pltpu.VMEM(atom_input.shape, BF16),
            pltpu.VMEM(pair_input.shape, BF16),
            pltpu.VMEM(tri_projection.shape, BF16),
            pltpu.VMEM(tri_gate_weight.shape, BF16),
            pltpu.VMEM(tri_out_weight.shape, BF16),
            pltpu.VMEM(pair_bias_weight.shape[::-1], BF16),
            pltpu.VMEM((total_atoms // LANES + 16, LANES), jnp.int32),
            pltpu.VMEM(atom_in_weight.shape, BF16),
            pltpu.VMEM(atom_out_weight.shape, BF16),
            pltpu.VMEM(pair_input.shape, BF16),
            pltpu.VMEM((chunks, width * rows, LANES), F32),
            pltpu.VMEM((chunks, width * rows, LANES), F32),
            pltpu.VMEM((groups, count, 2 * part, tokens), BF16),
            pltpu.VMEM((groups, count, 2 * part, tokens), BF16),
            pltpu.VMEM((groups, count, part, tokens), BF16),
            pltpu.VMEM((groups, count, part, tokens), BF16),
            pltpu.VMEM((rows, tokens, width), F32),
            pltpu.VMEM((atoms + 2 * RIM, width), BF16),
            pltpu.SemaphoreType.DMA((groups,)),
            pltpu.SemaphoreType.DMA((groups,)),
            pltpu.SemaphoreType.DMA((groups,)),
            pltpu.SemaphoreType.DMA((groups,)),
            pltpu.SemaphoreType.DMA((2,)),
            pltpu.SemaphoreType.DMA((2,)),
            pltpu.SemaphoreType.DMA((9,)),
            pltpu.SemaphoreType.DMA((rows + 1,)),
        ],
        compiler_params=pltpu.CompilerParams(
            collective_id=0, has_side_effects=True, vmem_limit_bytes=60 * 1024 * 1024
        ),
    )(
        pair_input,
        tri_projection,
        tri_gate_weight,
        tri_out_weight,
        pair_bias_weight.T,
        atom_input,
        atom_tokens.reshape(-1, LANES),
        atom_in_weight,
        atom_out_weight,
    )


def solution(mesh):
    placed = (
        P(("group", "row"), None, None),
        P(),
        P(),
        P(),
        P(),
        P(("group", "row"), None),
        P("group"),
        P(),
        P(),
    )
    return jax.shard_map(
        functools.partial(per_device, mesh.shape["row"]),
        mesh=mesh,
        in_specs=placed,
        out_specs=(P(("group", "row"), None, None), P(("group", "row"), None)),
        check_vma=False,
    )
```
